32 devices in a mesh: ctx: 16 (over z, x, core), head: 2 (over y).
Axes of the slice: x: 2, y: 2, z: 4, core: 2. Of those that a mesh axis runs over, the one named last changes fastest.
Arguments:
- query_nope: bfloat16 [2048, 16384], P('ctx', 'head'), may hold values from -6 to 6
- query_rope: bfloat16 [2048, 8192], P('ctx', 'head'), may hold values from -80 to 80
- out_grad: bfloat16 [2048, 16384], P('ctx', 'head'), may hold values from -6 to 6
- latent_codes: bfloat16 [2048, 512], P('ctx'), may hold values from -4 to 4
- scale_exponents: int32 [2048, 4], P('ctx'), may hold values from -2 to 1
- key_rope: bfloat16 [2048, 64], P('ctx'), may hold values from -2 to 2
- block_order: int32 [16], P('ctx'), may hold values from 0 to 15, each once
- up_keys: bfloat16 [128, 512, 128], P('head'), may hold values from -0.25 to 0.25
- up_values: bfloat16 [128, 512, 128], P('head'), may hold values from -0.25 to 0.25
Outputs:
- grad_query_nope: bfloat16 [2048, 16384], P('ctx', 'head')
- grad_query_rope: bfloat16 [2048, 8192], P('ctx', 'head')
- grad_latent: float32 [2048, 512], P('ctx')
- grad_key_rope: float32 [2048, 64], P('ctx')
The draws below stay inside these ranges and needn't reach their ends.
All inputs are finite; a program needn't handle non-finite values.
Results may differ from the reference program's by a relative error of at most 0.0097.
Values may be sent and summed in bfloat16 or wider, within the bound.
A program may use at most 192 MiB of HBM per device.

```python
import math
import jax
import jax.numpy as jnp
from jax import lax

HEADS = 128
LAT = 512
DR = 64
DN = 128
DV = 128
SB = 128
STEPS = 4
TOK_DEV = 128
TOKENS = 2048
N_CTX = 16


def rope_anchor(key):
    inner = jax.random.fold_in(key, 11)
    return jax.random.uniform(inner, (TOKENS, DR), jnp.float32, -2.0, 2.0)


def draw_key_rope(key, part):
    anchor = rope_anchor(key)
    return anchor.astype(jnp.bfloat16)


def draw_query_rope(key, part):
    key = jax.random.fold_in(key, 5)
    filled = jnp.clip(jax.random.normal(key, (TOKENS, HEADS, DR), jnp.float32), -4.0, 4.0)
    return filled.reshape(TOKENS, HEADS * DR).astype(jnp.bfloat16)


def touch_ends(entries, stream_key, smallest, high):
    extent = entries.shape
    index_at = [jax.random.randint(jax.random.fold_in(stream_key, axis), (), 0, extent[axis]) for axis in range(len(extent))]
    entries = entries.at[tuple(index_at)].set(smallest)
    longest = extent.index(max(extent))
    index_at[longest] = (index_at[longest] + 1) % extent[longest]
    return entries.at[tuple(index_at)].set(high)


def level_of(key, shape, pieces, smallest, high):
    level = 1.0
    for axis_at, shards_of in pieces:
        steps = jax.random.uniform(jax.random.fold_in(jax.random.fold_in(key, 6), axis_at), (shards_of,), jnp.float32, smallest / len(pieces), high / len(pieces))
        level = level * jnp.repeat(jnp.exp(steps), shape[axis_at] // shards_of).reshape((-1,) + (1,) * (len(shape) - 1 - axis_at))
    return level


def noise(stream_key, extent, deviation, reach, shards=(), held_as=jnp.bfloat16):
    level = level_of(stream_key, extent, shards, -0.22, 0.18) if shards else 1.0
    entries = jax.random.normal(stream_key, extent, jnp.float32) * deviation * level
    return jnp.minimum(jnp.maximum(entries, -reach), reach).astype(held_as)


def setup_inputs(seed: int = 0) -> dict:
    splits = jax.random.split(jax.random.key(seed), 10)
    query_nope = noise(splits[0], (TOKENS, HEADS * DN), 1.0, 6.0, ((0, 16), (1, 2)))
    query_rope = draw_query_rope(jax.random.fold_in(splits[9], 71), 0)
    out_grad = noise(splits[2], (TOKENS, HEADS * DV), 1.0, 6.0, ((0, 16), (1, 2)))
    latent_codes = noise(splits[3], (TOKENS, LAT), 1.0, 4.0, ((0, 16),))
    scale_exponents = touch_ends(jax.random.randint(splits[4], (TOKENS, LAT // SB), -2, 2), jax.random.fold_in(splits[4], 1), -2, 1).astype(jnp.int32)
    key_rope = draw_key_rope(jax.random.fold_in(splits[9], 71), 0)
    block_order = jax.random.permutation(splits[6], N_CTX).astype(jnp.int32)
    up_keys = noise(splits[7], (HEADS, LAT, DN), LAT ** -0.5, 0.25, ((0, 2),))
    up_values = noise(splits[8], (HEADS, LAT, DV), LAT ** -0.5, 0.25, ((0, 2),))
    return dict(query_nope=query_nope, query_rope=query_rope, out_grad=out_grad, latent_codes=latent_codes, scale_exponents=scale_exponents, key_rope=key_rope, block_order=block_order, up_keys=up_keys, up_values=up_values)


def rounded(tensor):
    return lax.optimization_barrier(tensor.astype(jnp.bfloat16)).astype(jnp.float32)

def dequantize(latent_codes, scale_exponents):
    factor = jnp.exp2(scale_exponents.astype(jnp.float32))
    widened = jnp.repeat(factor, latent_codes.shape[1] // scale_exponents.shape[1], axis=1)
    return (latent_codes.astype(jnp.float32) * widened).astype(jnp.bfloat16)

def reference(query_nope, query_rope, out_grad, latent_codes, scale_exponents, key_rope, block_order, up_keys, up_values):
    factor = 1.0 / math.sqrt(DN + DR)
    latent = dequantize(latent_codes, scale_exponents).astype(jnp.float32)
    key_nope = jnp.einsum('tc,hcd->thd', latent, up_keys.astype(jnp.float32)).astype(jnp.bfloat16)
    value_rows = jnp.einsum('tc,hcd->thd', latent, up_values.astype(jnp.float32)).astype(jnp.bfloat16)
    key_nope = key_nope.reshape(N_CTX, TOK_DEV, HEADS, DN)
    value_rows = value_rows.reshape(N_CTX, TOK_DEV, HEADS, DV)
    rope_keys = key_rope.reshape(N_CTX, TOK_DEV, DR)
    query_blocks = query_nope.reshape(N_CTX, TOK_DEV, HEADS, DN)
    rope_queries = query_rope.reshape(N_CTX, TOK_DEV, HEADS, DR)
    grad_blocks = out_grad.reshape(N_CTX, TOK_DEV, HEADS, DV)
    offsets = jnp.arange(STEPS, dtype=jnp.int32)
    within = jnp.arange(TOK_DEV, dtype=jnp.int32)

    def one_block(index):
        sources = ((index - offsets) % N_CTX).astype(jnp.int32)
        keys_here = key_nope[sources].reshape(STEPS * TOK_DEV, HEADS, DN).astype(jnp.float32)
        values_here = value_rows[sources].reshape(STEPS * TOK_DEV, HEADS, DV).astype(jnp.float32)
        rope_here = rope_keys[sources].reshape(STEPS * TOK_DEV, DR).astype(jnp.float32)
        key_position = (block_order[sources][:, None] * TOK_DEV + within[None, :]).reshape(-1)
        query_position = block_order[index] * TOK_DEV + within
        visible = key_position[None, :] <= query_position[:, None]
        queries = query_blocks[index].astype(jnp.float32)
        rope_query = rope_queries[index].astype(jnp.float32)
        grads = grad_blocks[index].astype(jnp.float32)
        score = factor * (jnp.einsum('thd,uhd->htu', queries, keys_here) + jnp.einsum('thr,ur->htu', rope_query, rope_here))
        score = jnp.where(visible[None], score, -jnp.inf)
        largest = lax.optimization_barrier(jnp.max(score, axis=2))
        expo = jnp.exp(score - largest[:, :, None])
        total = lax.optimization_barrier(jnp.sum(expo, axis=2))
        output = jnp.einsum('htu,uhv->htv', rounded(expo), values_here) / total[:, :, None]
        lse = largest + jnp.log(total)
        delta = lax.optimization_barrier(jnp.sum(jnp.transpose(grads, (1, 0, 2)) * output, axis=2))
        probs = jnp.exp(score - lse[:, :, None])
        grad_probs = jnp.einsum('thv,uhv->htu', grads, values_here)
        grad_score = rounded(probs * (grad_probs - delta[:, :, None]))
        probs_low = rounded(probs)
        grad_nope = factor * jnp.einsum('htu,uhd->thd', grad_score, keys_here)
        grad_rope = factor * jnp.einsum('htu,ur->thr', grad_score, rope_here)
        grad_keys = rounded(factor * jnp.einsum('htu,thd->uhd', grad_score, queries))
        grad_values = rounded(jnp.einsum('htu,thv->uhv', probs_low, grads))
        rope_part = factor * jnp.einsum('htu,thr->ur', grad_score, rope_query)
        latent_part = jnp.einsum('uhd,hcd->uc', grad_keys, up_keys.astype(jnp.float32)) + jnp.einsum('uhv,hcv->uc', grad_values, up_values.astype(jnp.float32))
        return (grad_nope.astype(jnp.bfloat16), grad_rope.astype(jnp.bfloat16), latent_part.reshape(STEPS, TOK_DEV, LAT), rope_part.reshape(STEPS, TOK_DEV, DR))
    outputs = lax.map(one_block, jnp.arange(N_CTX, dtype=jnp.int32))
    targets = ((jnp.arange(N_CTX, dtype=jnp.int32)[:, None] - offsets[None, :]) % N_CTX).reshape(-1).astype(jnp.int32)
    grad_latent = jnp.zeros((N_CTX, TOK_DEV, LAT), jnp.float32).at[targets].add(outputs[2].reshape(-1, TOK_DEV, LAT))
    grad_key_rope = jnp.zeros((N_CTX, TOK_DEV, DR), jnp.float32).at[targets].add(outputs[3].reshape(-1, TOK_DEV, DR))
    return (outputs[0].reshape(TOKENS, HEADS * DN), outputs[1].reshape(TOKENS, HEADS * DR), grad_latent.reshape(TOKENS, LAT), grad_key_rope.reshape(TOKENS, DR))
```

```python
import functools
import math

import jax
import jax.numpy as jnp
from jax import lax
from jax.experimental import pallas as pl
from jax.experimental.pallas import tpu as pltpu
from jax.sharding import PartitionSpec as P

STEPS = 4
F32 = jnp.float32
BF16 = jnp.bfloat16


def shifted(block, axis, distance):
    devices = range(lax.axis_size(axis))
    route = [((i - distance) % len(devices), i) for i in devices]
    return lax.ppermute(block, axis, route)


def nt(a, b):
    return lax.dot_general(a, b, (((1,), (1,)), ((), ())), preferred_element_type=F32)


def nn(a, b):
    return lax.dot_general(a, b, (((1,), (0,)), ((), ())), preferred_element_type=F32)


def tn(a, b):
    return lax.dot_general(a, b, (((0,), (0,)), ((), ())), preferred_element_type=F32)


def attend(
    dims,
    pack0,
    pack1,
    pack2,
    pack3,
    q_ref,
    qr_ref,
    g_ref,
    uk_ref,
    uv_ref,
    dq_ref,
    dqr_ref,
    dlat_ref,
    drope_ref,
    lat,
    rope_even,
    rope_odd,
    bias,
):
    tokens, width, nope, rope, group = dims
    step = pl.program_id(0)
    factor = 1.0 / math.sqrt(nope + rope)
    log2_scale = factor * math.log2(math.e)

    @pl.when(step == 0)
    def _():
        lane = lax.broadcasted_iota(jnp.int32, (tokens, 2 * rope), 1)
        row = lax.broadcasted_iota(jnp.int32, (tokens, tokens), 0).astype(F32)
        col = lax.broadcasted_iota(jnp.int32, (tokens, tokens), 1).astype(F32)
        own = None
        for s, pack in enumerate((pack0, pack1, pack2, pack3)):
            rows = pl.ds(s * tokens, tokens)
            lat[rows, :] = pack[:, :width]
            tail = pack[:, width:].astype(F32)
            turned = pltpu.roll(tail, rope, 1)
            rope_even[rows, :] = jnp.where(lane < rope, tail, 0.0).astype(BF16)
            rope_odd[rows, :] = jnp.where(lane >= rope, turned, 0.0).astype(BF16)
            place = jnp.broadcast_to(tail[:, rope : rope + 1], (tokens, tokens)) * tokens
            if s == 0:
                own = place
            bias[rows, :] = jnp.where(place + row <= own + col, 0.0, -jnp.inf)
        dlat_ref[...] = jnp.zeros_like(dlat_ref)
        drope_ref[...] = jnp.zeros_like(drope_ref)

    latent = lat[...]
    lane_q = lax.broadcasted_iota(jnp.int32, (tokens, 2 * rope), 1)
    for pair in range(group // 2):
        first, second = 2 * pair, 2 * pair + 1
        qr = qr_ref[:, pair * 2 * rope : (pair + 1) * 2 * rope]
        keys = nn(latent, jnp.concatenate([uk_ref[first], uk_ref[second]], axis=1)).astype(BF16)
        q = [q_ref[:, h * nope : (h + 1) * nope] for h in (first, second)]
        g = [g_ref[:, h * nope : (h + 1) * nope] for h in (first, second)]
        q_lat = [(nt(q[i], uk_ref[h]) * factor).astype(BF16) for i, h in enumerate((first, second))]
        g_lat = [nt(g[i], uv_ref[h]).astype(BF16) for i, h in enumerate((first, second))]
        dp_both = nt(latent, jnp.concatenate(g_lat, axis=0))
        left = []
        right = []
        turned = None
        scores = []
        for i in range(2):
            full_keys = jnp.concatenate(
                [keys[:, i * nope : (i + 1) * nope], (rope_even, rope_odd)[i][...]], axis=1
            )
            raw = nt(full_keys, jnp.concatenate([q[i], qr], axis=1))
            score = raw * log2_scale + bias[...]
            top = jnp.max(score, axis=0, keepdims=True)
            weight = jnp.exp2(score - top)
            inverse = 1.0 / jnp.sum(weight, axis=0, keepdims=True)
            dp = dp_both[:, i * tokens : (i + 1) * tokens]
            delta = jnp.sum(weight * dp, axis=0, keepdims=True) * inverse
            prob = weight * inverse
            ds = (prob * (dp - delta)).astype(BF16)
            scores.append(ds)
            left += [ds, prob.astype(BF16)]
            right += [q_lat[i], g_lat[i]]
            grad = tn(ds, full_keys) * factor
            h = (first, second)[i]
            dq_ref[:, h * nope : (h + 1) * nope] = grad[:, :nope].astype(BF16)
            turned = grad[:, nope:] if turned is None else turned + grad[:, nope:]
        dqr_ref[:, pair * 2 * rope : (pair + 1) * 2 * rope] = turned.astype(BF16)
        dlat_ref[...] += nn(jnp.concatenate(left, axis=1), jnp.concatenate(right, axis=0))
        zero = jnp.zeros_like(qr)
        qr_split = jnp.concatenate(
            [jnp.where(lane_q < rope, qr, zero), jnp.where(lane_q >= rope, qr, zero)], axis=0
        )
        drope_ref[...] += nn(jnp.concatenate(scores, axis=1), qr_split)


def body(
    query_nope,
    query_rope,
    out_grad,
    latent_codes,
    scale_exponents,
    key_rope,
    block_order,
    up_keys,
    up_values,
):
    tokens, width = latent_codes.shape
    heads, _, nope = up_keys.shape
    rope = key_rope.shape[1]
    group = 4
    factor = 1.0 / math.sqrt(nope + rope)
    scale = jnp.exp2(scale_exponents.astype(F32))
    widened = jnp.repeat(scale, width // scale_exponents.shape[1], axis=1)
    latent = (latent_codes.astype(F32) * widened).astype(BF16)
    place = jnp.broadcast_to(block_order.astype(BF16)[None, :], (tokens, rope))
    pack = jnp.concatenate([latent, key_rope, place], axis=1)
    packs = [pack] + [shifted(pack, "ctx", s) for s in range(1, STEPS)]
    keys = STEPS * tokens
    whole = lambda i: (0, 0)
    cols = lambda i: (0, i)
    per_head = lambda i: (i, 0, 0)
    grad_nope, grad_rope, dlat, drope = pl.pallas_call(
        functools.partial(attend, (tokens, width, nope, rope, group)),
        grid=(heads // group,),
        in_specs=[pl.BlockSpec((tokens, width + 2 * rope), whole)] * STEPS
        + [
            pl.BlockSpec((tokens, group * nope), cols),
            pl.BlockSpec((tokens, group * rope), cols),
            pl.BlockSpec((tokens, group * nope), cols),
            pl.BlockSpec((group, width, nope), per_head),
            pl.BlockSpec((group, width, nope), per_head),
        ],
        out_specs=[
            pl.BlockSpec((tokens, group * nope), cols),
            pl.BlockSpec((tokens, group * rope), cols),
            pl.BlockSpec((keys, width), whole),
            pl.BlockSpec((keys, 2 * rope), whole),
        ],
        out_shape=[
            jax.ShapeDtypeStruct((tokens, heads * nope), BF16),
            jax.ShapeDtypeStruct((tokens, heads * rope), BF16),
            jax.ShapeDtypeStruct((keys, width), F32),
            jax.ShapeDtypeStruct((keys, 2 * rope), F32),
        ],
        scratch_shapes=[
            pltpu.VMEM((keys, width), BF16),
            pltpu.VMEM((keys, 2 * rope), BF16),
            pltpu.VMEM((keys, 2 * rope), BF16),
            pltpu.VMEM((keys, tokens), F32),
        ],
        compiler_params=pltpu.CompilerParams(
            dimension_semantics=("arbitrary",), vmem_limit_bytes=48 * 2**20
        ),
    )(*packs, query_nope, query_rope, out_grad, up_keys, up_values)
    drope = (drope[:, :rope] + drope[:, rope:]) * factor
    both = jnp.concatenate([dlat, drope], axis=1).reshape(STEPS, tokens, width + rope)
    total = both[0]
    for s in range(1, STEPS):
        total = total + shifted(both[s].astype(BF16), "ctx", -s).astype(F32)
    total = lax.psum(total.astype(BF16), "head").astype(F32)
    return (grad_nope, grad_rope, total[:, :width], total[:, width:])


def solution(mesh):
    return jax.shard_map(
        body,
        mesh=mesh,
        in_specs=(
            P("ctx", "head"),
            P("ctx", "head"),
            P("ctx", "head"),
            P("ctx", None),
            P("ctx", None),
            P("ctx", None),
            P("ctx"),
            P("head", None, None),
            P("head", None, None),
        ),
        out_specs=(P("ctx", "head"), P("ctx", "head"), P("ctx", None), P("ctx", None)),
        check_vma=False,
    )
```

```python
import functools
import math

import jax
import jax.numpy as jnp
from jax import lax
from jax.experimental import pallas as pl
from jax.experimental.pallas import tpu as pltpu
from jax.sharding import PartitionSpec as P

STEPS = 4
F32 = jnp.float32
BF16 = jnp.bfloat16
MESH = pl.DeviceIdType.MESH


def nt(a, b):
    return lax.dot_general(a, b, (((1,), (1,)), ((), ())), preferred_element_type=F32)


def nn(a, b):
    return lax.dot_general(a, b, (((1,), (0,)), ((), ())), preferred_element_type=F32)


def tn(a, b):
    return lax.dot_general(a, b, (((0,), (0,)), ((), ())), preferred_element_type=F32)

def wrapped(index, size):
    return lax.rem(index + size, size)


def greet(ring, heads_axis):
    barrier = pltpu.get_barrier_semaphore()
    me = lax.axis_index("ctx")
    count = 0
    for s in range(1, STEPS):
        for other in (me + s, me - s):
            pl.semaphore_signal(
                barrier, inc=1, device_id={"ctx": wrapped(other, ring)}, device_id_type=MESH
            )
            count += 1
    mine = lax.axis_index("head")
    for j in range(1, heads_axis):
        pl.semaphore_signal(
            barrier,
            inc=1,
            device_id={"head": lax.rem(mine + j, heads_axis)},
            device_id_type=MESH,
        )
        count += 1
    pl.semaphore_wait(barrier, count)


def collect(ring, codes_ref, exps_ref, rope_ref, order_ref, out, send_sem, recv_sem):
    tokens, width = codes_ref.shape
    rope = rope_ref.shape[1]
    groups = exps_ref.shape[1]
    part = width // groups
    exps = exps_ref[...]
    scale = jnp.where(
        exps == -2, 0.25, jnp.where(exps == -1, 0.5, jnp.where(exps == 0, 1.0, 2.0))
    ).astype(F32)
    for j in range(groups):
        span = slice(j * part, (j + 1) * part)
        out[0, :, span] = (codes_ref[:, span].astype(F32) * scale[:, j : j + 1]).astype(BF16)
    place = jnp.full((tokens, rope), order_ref[0], jnp.int32).astype(F32)
    out[0, :, width:] = jnp.concatenate([rope_ref[...].astype(F32), place], axis=1).astype(BF16)
    greet(ring, 1)
    me = lax.axis_index("ctx")
    copies = []
    for s in (3, 2, 1):
        copy = pltpu.make_async_remote_copy(
            src_ref=out.at[0],
            dst_ref=out.at[s],
            send_sem=send_sem.at[s],
            recv_sem=recv_sem.at[s],
            device_id={"ctx": wrapped(me + s, ring)},
            device_id_type=MESH,
        )
        copy.start()
        copies.append(copy)
    for copy in copies:
        copy.wait()


def bring_home(
    sizes,
    dlat_ref,
    drope_ref,
    latent_out,
    rope_out,
    parts,
    landed,
    summed,
    send_sem,
    recv_sem,
    head_send,
    head_recv,
):
    ring, heads_axis, factor = sizes
    tokens, width = latent_out.shape
    rope = rope_out.shape[1]
    me = lax.axis_index("ctx")
    mine = lax.axis_index("head")
    for s in range(1, STEPS):
        rows = pl.ds(s * tokens, tokens)
        parts[s, :, :width] = dlat_ref[rows, :].astype(BF16)
        parts[s, :, width:] = drope_ref[rows, :].astype(BF16)
    greet(ring, heads_axis)
    copies = []
    for s in (3, 2, 1):
        copy = pltpu.make_async_remote_copy(
            src_ref=parts.at[s],
            dst_ref=landed.at[s],
            send_sem=send_sem.at[s],
            recv_sem=recv_sem.at[s],
            device_id={"ctx": wrapped(me - s, ring)},
            device_id_type=MESH,
        )
        copy.start()
        copies.append(copy)
    for copy in copies:
        copy.wait()
    lat_total = dlat_ref[:tokens, :]
    rope_total = drope_ref[:tokens, :]
    for s in range(1, STEPS):
        lat_total = lat_total + landed[s, :, :width].astype(F32)
        rope_total = rope_total + landed[s, :, width:].astype(F32)
    summed[mine, :, :width] = lat_total.astype(BF16)
    summed[mine, :, width:] = rope_total.astype(BF16)
    copies = []
    for j in range(1, heads_axis):
        copy = pltpu.make_async_remote_copy(
            src_ref=summed.at[mine],
            dst_ref=summed.at[mine],
            send_sem=head_send.at[j],
            recv_sem=head_recv.at[j],
            device_id={"head": lax.rem(mine + j, heads_axis)},
            device_id_type=MESH,
        )
        copy.start()
        copies.append(copy)
    for copy in copies:
        copy.wait()
    total = summed[0].astype(F32)
    for j in range(1, heads_axis):
        total = total + summed[j].astype(F32)
    latent_out[...] = total[:, :width]
    rope_out[...] = (total[:, width : width + rope] + total[:, width + rope :]) * factor


def attend(
    dims,
    packs,
    q_ref,
    qr_ref,
    g_ref,
    uk_ref,
    uv_ref,
    dq_ref,
    dqr_ref,
    dlat_ref,
    drope_ref,
    lat,
    rope_even,
    rope_odd,
    bias,
):
    tokens, width, nope, rope, group = dims
    step = pl.program_id(0)
    factor = 1.0 / math.sqrt(nope + rope)
    log2_scale = factor * math.log2(math.e)

    @pl.when(step == 0)
    def _():
        lane = lax.broadcasted_iota(jnp.int32, (tokens, 2 * rope), 1)
        row = lax.broadcasted_iota(jnp.int32, (tokens, tokens), 0).astype(F32)
        col = lax.broadcasted_iota(jnp.int32, (tokens, tokens), 1).astype(F32)
        own = None
        for s in range(STEPS):
            rows = pl.ds(s * tokens, tokens)
            lat[rows, :] = packs[s, :, :width]
            tail = packs[s, :, width:].astype(F32)
            turned = pltpu.roll(tail, rope, 1)
            rope_even[rows, :] = jnp.where(lane < rope, tail, 0.0).astype(BF16)
            rope_odd[rows, :] = jnp.where(lane >= rope, turned, 0.0).astype(BF16)
            place = jnp.broadcast_to(tail[:, rope : rope + 1], (tokens, tokens)) * tokens
            if s == 0:
                own = place
            bias[rows, :] = jnp.where(place + row <= own + col, 0.0, -jnp.inf)
        dlat_ref[...] = jnp.zeros_like(dlat_ref)
        drope_ref[...] = jnp.zeros_like(drope_ref)

    latent = lat[...]
    lane_q = lax.broadcasted_iota(jnp.int32, (tokens, 2 * rope), 1)
    for pair in range(group // 2):
        first, second = 2 * pair, 2 * pair + 1
        qr = qr_ref[:, pair * 2 * rope : (pair + 1) * 2 * rope]
        keys = nn(latent, jnp.concatenate([uk_ref[first], uk_ref[second]], axis=1)).astype(BF16)
        q = [q_ref[:, h * nope : (h + 1) * nope] for h in (first, second)]
        g = [g_ref[:, h * nope : (h + 1) * nope] for h in (first, second)]
        q_lat = [(nt(q[i], uk_ref[h]) * factor).astype(BF16) for i, h in enumerate((first, second))]
        g_lat = [nt(g[i], uv_ref[h]).astype(BF16) for i, h in enumerate((first, second))]
        dp_both = nt(latent, jnp.concatenate(g_lat, axis=0))
        left = []
        right = []
        turned = None
        scores = []
        for i in range(2):
            full_keys = jnp.concatenate(
                [keys[:, i * nope : (i + 1) * nope], (rope_even, rope_odd)[i][...]], axis=1
            )
            raw = nt(full_keys, jnp.concatenate([q[i], qr], axis=1))
            score = raw * log2_scale + bias[...]
            top = jnp.max(score, axis=0, keepdims=True)
            weight = jnp.exp2(score - top)
            inverse = 1.0 / jnp.sum(weight, axis=0, keepdims=True)
            dp = dp_both[:, i * tokens : (i + 1) * tokens]
            delta = jnp.sum(weight * dp, axis=0, keepdims=True) * inverse
            prob = weight * inverse
            ds = (prob * (dp - delta)).astype(BF16)
            scores.append(ds)
            left += [ds, prob.astype(BF16)]
            right += [q_lat[i], g_lat[i]]
            grad = tn(ds, full_keys) * factor
            h = (first, second)[i]
            dq_ref[:, h * nope : (h + 1) * nope] = grad[:, :nope].astype(BF16)
            turned = grad[:, nope:] if turned is None else turned + grad[:, nope:]
        dqr_ref[:, pair * 2 * rope : (pair + 1) * 2 * rope] = turned.astype(BF16)
        dlat_ref[...] += nn(jnp.concatenate(left, axis=1), jnp.concatenate(right, axis=0))
        zero = jnp.zeros_like(qr)
        qr_split = jnp.concatenate(
            [jnp.where(lane_q < rope, qr, zero), jnp.where(lane_q >= rope, qr, zero)], axis=0
        )
        drope_ref[...] += nn(jnp.concatenate(scores, axis=1), qr_split)


def body(
    query_nope,
    query_rope,
    out_grad,
    latent_codes,
    scale_exponents,
    key_rope,
    block_order,
    up_keys,
    up_values,
):
    tokens, width = latent_codes.shape
    heads, _, nope = up_keys.shape
    rope = key_rope.shape[1]
    group = 4
    factor = 1.0 / math.sqrt(nope + rope)
    ring = lax.axis_size("ctx")
    heads_axis = lax.axis_size("head")
    vmem = pl.BlockSpec(memory_space=pltpu.VMEM)
    packs = pl.pallas_call(
        functools.partial(collect, ring),
        out_shape=jax.ShapeDtypeStruct((STEPS, tokens, width + 2 * rope), BF16),
        in_specs=[vmem] * 3 + [pl.BlockSpec(memory_space=pltpu.SMEM)],
        out_specs=vmem,
        scratch_shapes=[pltpu.SemaphoreType.DMA((STEPS,)), pltpu.SemaphoreType.DMA((STEPS,))],
        compiler_params=pltpu.CompilerParams(collective_id=0, has_side_effects=True),
    )(latent_codes, scale_exponents, key_rope, block_order)
    keys = STEPS * tokens
    whole = lambda i: (0, 0)
    cols = lambda i: (0, i)
    per_head = lambda i: (i, 0, 0)
    grad_nope, grad_rope, dlat, drope = pl.pallas_call(
        functools.partial(attend, (tokens, width, nope, rope, group)),
        grid=(heads // group,),
        in_specs=[pl.BlockSpec((STEPS, tokens, width + 2 * rope), lambda i: (0, 0, 0))]
        + [
            pl.BlockSpec((tokens, group * nope), cols),
            pl.BlockSpec((tokens, group * rope), cols),
            pl.BlockSpec((tokens, group * nope), cols),
            pl.BlockSpec((group, width, nope), per_head),
            pl.BlockSpec((group, width, nope), per_head),
        ],
        out_specs=[
            pl.BlockSpec((tokens, group * nope), cols),
            pl.BlockSpec((tokens, group * rope), cols),
            pl.BlockSpec((keys, width), whole),
            pl.BlockSpec((keys, 2 * rope), whole),
        ],
        out_shape=[
            jax.ShapeDtypeStruct((tokens, heads * nope), BF16),
            jax.ShapeDtypeStruct((tokens, heads * rope), BF16),
            jax.ShapeDtypeStruct((keys, width), F32),
            jax.ShapeDtypeStruct((keys, 2 * rope), F32),
        ],
        scratch_shapes=[
            pltpu.VMEM((keys, width), BF16),
            pltpu.VMEM((keys, 2 * rope), BF16),
            pltpu.VMEM((keys, 2 * rope), BF16),
            pltpu.VMEM((keys, tokens), F32),
        ],
        compiler_params=pltpu.CompilerParams(
            dimension_semantics=("arbitrary",), vmem_limit_bytes=48 * 2**20
        ),
    )(packs, query_nope, query_rope, out_grad, up_keys, up_values)
    block = (tokens, width + 2 * rope)
    grad_latent, grad_rope_keys = pl.pallas_call(
        functools.partial(bring_home, (ring, heads_axis, factor)),
        out_shape=[
            jax.ShapeDtypeStruct((tokens, width), F32),
            jax.ShapeDtypeStruct((tokens, rope), F32),
        ],
        in_specs=[vmem, vmem],
        out_specs=[vmem, vmem],
        scratch_shapes=[
            pltpu.VMEM((STEPS,) + block, BF16),
            pltpu.VMEM((STEPS,) + block, BF16),
            pltpu.VMEM((heads_axis,) + block, BF16),
            pltpu.SemaphoreType.DMA((STEPS,)),
            pltpu.SemaphoreType.DMA((STEPS,)),
            pltpu.SemaphoreType.DMA((heads_axis,)),
            pltpu.SemaphoreType.DMA((heads_axis,)),
        ],
        compiler_params=pltpu.CompilerParams(
            collective_id=1, has_side_effects=True, vmem_limit_bytes=16 * 2**20
        ),
    )(dlat, drope)
    return (grad_nope, grad_rope, grad_latent, grad_rope_keys)


def solution(mesh):
    return jax.shard_map(
        body,
        mesh=mesh,
        in_specs=(
            P("ctx", "head"),
            P("ctx", "head"),
            P("ctx", "head"),
            P("ctx", None),
            P("ctx", None),
            P("ctx", None),
            P("ctx"),
            P("head", None, None),
            P("head", None, None),
        ),
        out_specs=(P("ctx", "head"), P("ctx", "head"), P("ctx", None), P("ctx", None)),
        check_vma=False,
    )
```

```python
import functools
import math

import jax
import jax.numpy as jnp
from jax import lax
from jax.experimental import pallas as pl
from jax.experimental.pallas import tpu as pltpu
from jax.sharding import PartitionSpec as P

STEPS = 4
F32 = jnp.float32
BF16 = jnp.bfloat16
MESH = pl.DeviceIdType.MESH


def nt(a, b):
    return lax.dot_general(a, b, (((1,), (1,)), ((), ())), preferred_element_type=F32)


def nn(a, b):
    return lax.dot_general(a, b, (((1,), (0,)), ((), ())), preferred_element_type=F32)


def tn(a, b):
    return lax.dot_general(a, b, (((0,), (0,)), ((), ())), preferred_element_type=F32)

def wrapped(index, size):
    return lax.rem(index + size, size)


def greet(ring, heads_axis):
    barrier = pltpu.get_barrier_semaphore()
    me = lax.axis_index("ctx")
    count = 0
    for s in range(1, STEPS):
        for other in (me + s, me - s):
            pl.semaphore_signal(
                barrier, inc=1, device_id={"ctx": wrapped(other, ring)}, device_id_type=MESH
            )
            count += 1
    mine = lax.axis_index("head")
    for j in range(1, heads_axis):
        pl.semaphore_signal(
            barrier,
            inc=1,
            device_id={"head": lax.rem(mine + j, heads_axis)},
            device_id_type=MESH,
        )
        count += 1
    return lambda: pl.semaphore_wait(barrier, count)


def collect(ring, codes_ref, exps_ref, rope_ref, order_ref, out, send_sem, recv_sem):
    met = greet(ring, 1)
    tokens, width = codes_ref.shape
    rope = rope_ref.shape[0]
    groups = exps_ref.shape[0]
    part = width // groups
    exps = exps_ref[...]
    scale = jnp.where(
        exps == -2, 0.25, jnp.where(exps == -1, 0.5, jnp.where(exps == 0, 1.0, 2.0))
    ).astype(F32)
    scale = jnp.concatenate([scale, jnp.zeros((8 - groups, tokens), F32)], axis=0).T
    for j in range(groups):
        span = slice(j * part, (j + 1) * part)
        out[0, :, span] = (codes_ref[:, span].astype(F32) * scale[:, j : j + 1]).astype(BF16)
    place = jnp.full((tokens, rope), order_ref[0], jnp.int32).astype(F32)
    out[0, :, width:] = jnp.concatenate([rope_ref[...].astype(F32).T, place], axis=1).astype(BF16)
    met()
    me = lax.axis_index("ctx")
    copies = []
    for s in (3, 2, 1):
        copy = pltpu.make_async_remote_copy(
            src_ref=out.at[0],
            dst_ref=out.at[s],
            send_sem=send_sem.at[s],
            recv_sem=recv_sem.at[s],
            device_id={"ctx": wrapped(me + s, ring)},
            device_id_type=MESH,
        )
        copy.start()
        copies.append(copy)
    for copy in copies:
        copy.wait()


def bring_home(
    sizes,
    dlat_ref,
    drope_ref,
    latent_out,
    rope_out,
    parts,
    landed,
    summed,
    send_sem,
    recv_sem,
    head_send,
    head_recv,
):
    ring, heads_axis, factor = sizes
    met = greet(ring, heads_axis)
    tokens, width = latent_out.shape
    rope = rope_out.shape[0]
    me = lax.axis_index("ctx")
    mine = lax.axis_index("head")
    for s in range(1, STEPS):
        rows = pl.ds(s * tokens, tokens)
        parts[s, :, :width] = dlat_ref[rows, :].astype(BF16)
        parts[s, :, width:] = drope_ref[rows, :].astype(BF16)
    met()
    copies = []
    for s in (3, 2, 1):
        copy = pltpu.make_async_remote_copy(
            src_ref=parts.at[s],
            dst_ref=landed.at[s],
            send_sem=send_sem.at[s],
            recv_sem=recv_sem.at[s],
            device_id={"ctx": wrapped(me - s, ring)},
            device_id_type=MESH,
        )
        copy.start()
        copies.append(copy)
    for copy in copies:
        copy.wait()
    lat_total = dlat_ref[:tokens, :]
    rope_total = drope_ref[:tokens, :]
    for s in range(1, STEPS):
        lat_total = lat_total + landed[s, :, :width].astype(F32)
        rope_total = rope_total + landed[s, :, width:].astype(F32)
    summed[mine, :, :width] = lat_total.astype(BF16)
    summed[mine, :, width:] = rope_total.astype(BF16)
    copies = []
    for j in range(1, heads_axis):
        copy = pltpu.make_async_remote_copy(
            src_ref=summed.at[mine],
            dst_ref=summed.at[mine],
            send_sem=head_send.at[j],
            recv_sem=head_recv.at[j],
            device_id={"head": lax.rem(mine + j, heads_axis)},
            device_id_type=MESH,
        )
        copy.start()
        copies.append(copy)
    for copy in copies:
        copy.wait()
    total = summed[0].astype(F32)
    for j in range(1, heads_axis):
        total = total + summed[j].astype(F32)
    latent_out[...] = total[:, :width]
    tail = total[:, width:].T
    rope_out[...] = (tail[:rope] + tail[rope:]) * factor


def attend(
    dims,
    packs,
    q_ref,
    qr_ref,
    g_ref,
    uk_ref,
    uv_ref,
    dq_ref,
    dqr_ref,
    dlat_ref,
    drope_ref,
    lat,
    rope_even,
    rope_odd,
    bias,
):
    tokens, width, nope, rope, group = dims
    step = pl.program_id(0)
    factor = 1.0 / math.sqrt(nope + rope)
    log2_scale = factor * math.log2(math.e)

    @pl.when(step == 0)
    def _():
        lane = lax.broadcasted_iota(jnp.int32, (tokens, 2 * rope), 1)
        row = lax.broadcasted_iota(jnp.int32, (tokens, tokens), 0).astype(F32)
        col = lax.broadcasted_iota(jnp.int32, (tokens, tokens), 1).astype(F32)
        own = None
        for s in range(STEPS):
            rows = pl.ds(s * tokens, tokens)
            lat[rows, :] = packs[s, :, :width]
            tail = packs[s, :, width:].astype(F32)
            turned = pltpu.roll(tail, rope, 1)
            rope_even[rows, :] = jnp.where(lane < rope, tail, 0.0).astype(BF16)
            rope_odd[rows, :] = jnp.where(lane >= rope, turned, 0.0).astype(BF16)
            place = jnp.broadcast_to(tail[:, rope : rope + 1], (tokens, tokens)) * tokens
            if s == 0:
                own = place
            bias[rows, :] = jnp.where(place + row <= own + col, 0.0, -jnp.inf)
        dlat_ref[...] = jnp.zeros_like(dlat_ref)
        drope_ref[...] = jnp.zeros_like(drope_ref)

    latent = lat[...]
    lane_q = lax.broadcasted_iota(jnp.int32, (tokens, 2 * rope), 1)
    for pair in range(group // 2):
        first, second = 2 * pair, 2 * pair + 1
        qr = qr_ref[:, pair * 2 * rope : (pair + 1) * 2 * rope]
        keys = nn(latent, jnp.concatenate([uk_ref[first], uk_ref[second]], axis=1)).astype(BF16)
        q = [q_ref[:, h * nope : (h + 1) * nope] for h in (first, second)]
        g = [g_ref[:, h * nope : (h + 1) * nope] for h in (first, second)]
        q_lat = [(nt(uk_ref[h], q[i]) * factor).astype(BF16) for i, h in enumerate((first, second))]
        g_lat = [nt(uv_ref[h], g[i]).astype(BF16) for i, h in enumerate((first, second))]
        dp_both = nn(latent, jnp.concatenate(g_lat, axis=1))
        left = []
        right = []
        turned = None
        scores = []
        for i in range(2):
            full_keys = jnp.concatenate(
                [keys[:, i * nope : (i + 1) * nope], (rope_even, rope_odd)[i][...]], axis=1
            )
            raw = nt(full_keys, jnp.concatenate([q[i], qr], axis=1))
            score = raw * log2_scale + bias[...]
            top = jnp.max(score, axis=0, keepdims=True)
            weight = jnp.exp2(score - top)
            inverse = 1.0 / jnp.sum(weight, axis=0, keepdims=True)
            dp = dp_both[:, i * tokens : (i + 1) * tokens]
            delta = jnp.sum(weight * dp, axis=0, keepdims=True) * inverse
            prob = weight * inverse
            ds = (prob * (dp - delta)).astype(BF16)
            scores.append(ds)
            left += [ds, prob.astype(BF16)]
            right += [q_lat[i], g_lat[i]]
            grad = tn(full_keys, ds).T * factor
            h = (first, second)[i]
            dq_ref[:, h * nope : (h + 1) * nope] = grad[:, :nope].astype(BF16)
            turned = grad[:, nope:] if turned is None else turned + grad[:, nope:]
        dqr_ref[:, pair * 2 * rope : (pair + 1) * 2 * rope] = turned.astype(BF16)
        dlat_ref[...] += nt(jnp.concatenate(left, axis=1), jnp.concatenate(right, axis=1))
        zero = jnp.zeros_like(qr)
        qr_split = jnp.concatenate(
            [jnp.where(lane_q < rope, qr, zero), jnp.where(lane_q >= rope, qr, zero)], axis=0
        )
        drope_ref[...] += nn(jnp.concatenate(scores, axis=1), qr_split)


def body(
    query_nope,
    query_rope,
    out_grad,
    latent_codes,
    scale_exponents,
    key_rope,
    block_order,
    up_keys,
    up_values,
):
    tokens, width = latent_codes.shape
    heads, _, nope = up_keys.shape
    rope = key_rope.shape[1]
    group = 8
    factor = 1.0 / math.sqrt(nope + rope)
    ring = lax.axis_size("ctx")
    heads_axis = lax.axis_size("head")
    vmem = pl.BlockSpec(memory_space=pltpu.VMEM)
    packs = pl.pallas_call(
        functools.partial(collect, ring),
        out_shape=jax.ShapeDtypeStruct((STEPS, tokens, width + 2 * rope), BF16),
        in_specs=[vmem] * 3 + [pl.BlockSpec(memory_space=pltpu.SMEM)],
        out_specs=vmem,
        scratch_shapes=[pltpu.SemaphoreType.DMA((STEPS,)), pltpu.SemaphoreType.DMA((STEPS,))],
        compiler_params=pltpu.CompilerParams(collective_id=0, has_side_effects=True),
    )(latent_codes, scale_exponents.T, key_rope.T, block_order)
    keys = STEPS * tokens
    whole = lambda i: (0, 0)
    cols = lambda i: (0, i)
    per_head = lambda i: (i, 0, 0)
    grad_nope, grad_rope, dlat, drope = pl.pallas_call(
        functools.partial(attend, (tokens, width, nope, rope, group)),
        grid=(heads // group,),
        in_specs=[pl.BlockSpec((STEPS, tokens, width + 2 * rope), lambda i: (0, 0, 0))]
        + [
            pl.BlockSpec((tokens, group * nope), cols),
            pl.BlockSpec((tokens, group * rope), cols),
            pl.BlockSpec((tokens, group * nope), cols),
            pl.BlockSpec((group, width, nope), per_head),
            pl.BlockSpec((group, width, nope), per_head),
        ],
        out_specs=[
            pl.BlockSpec((tokens, group * nope), cols),
            pl.BlockSpec((tokens, group * rope), cols),
            pl.BlockSpec((keys, width), whole),
            pl.BlockSpec((keys, 2 * rope), whole),
        ],
        out_shape=[
            jax.ShapeDtypeStruct((tokens, heads * nope), BF16),
            jax.ShapeDtypeStruct((tokens, heads * rope), BF16),
            jax.ShapeDtypeStruct((keys, width), F32),
            jax.ShapeDtypeStruct((keys, 2 * rope), F32),
        ],
        scratch_shapes=[
            pltpu.VMEM((keys, width), BF16),
            pltpu.VMEM((keys, 2 * rope), BF16),
            pltpu.VMEM((keys, 2 * rope), BF16),
            pltpu.VMEM((keys, tokens), F32),
        ],
        compiler_params=pltpu.CompilerParams(
            dimension_semantics=("arbitrary",), vmem_limit_bytes=60 * 2**20
        ),
    )(packs, query_nope, query_rope, out_grad, up_keys, up_values)
    block = (tokens, width + 2 * rope)
    grad_latent, grad_rope_keys = pl.pallas_call(
        functools.partial(bring_home, (ring, heads_axis, factor)),
        out_shape=[
            jax.ShapeDtypeStruct((tokens, width), F32),
            jax.ShapeDtypeStruct((rope, tokens), F32),
        ],
        in_specs=[vmem, vmem],
        out_specs=[vmem, vmem],
        scratch_shapes=[
            pltpu.VMEM((STEPS,) + block, BF16),
            pltpu.VMEM((STEPS,) + block, BF16),
            pltpu.VMEM((heads_axis,) + block, BF16),
            pltpu.SemaphoreType.DMA((STEPS,)),
            pltpu.SemaphoreType.DMA((STEPS,)),
            pltpu.SemaphoreType.DMA((heads_axis,)),
            pltpu.SemaphoreType.DMA((heads_axis,)),
        ],
        compiler_params=pltpu.CompilerParams(
            collective_id=1, has_side_effects=True, vmem_limit_bytes=16 * 2**20
        ),
    )(dlat, drope)
    return (grad_nope, grad_rope, grad_latent, grad_rope_keys.T)


def solution(mesh):
    return jax.shard_map(
        body,
        mesh=mesh,
        in_specs=(
            P("ctx", "head"),
            P("ctx", "head"),
            P("ctx", "head"),
            P("ctx", None),
            P("ctx", None),
            P("ctx", None),
            P("ctx"),
            P("head", None, None),
            P("head", None, None),
        ),
        out_specs=(P("ctx", "head"), P("ctx", "head"), P("ctx", None), P("ctx", None)),
        check_vma=False,
    )
```

```python
import functools
import math

import jax
import jax.numpy as jnp
from jax import lax
from jax.experimental import pallas as pl
from jax.experimental.pallas import tpu as pltpu
from jax.sharding import PartitionSpec as P

STEPS = 4
F32 = jnp.float32
BF16 = jnp.bfloat16
MESH = pl.DeviceIdType.MESH


def nt(a, b):
    return lax.dot_general(a, b, (((1,), (1,)), ((), ())), preferred_element_type=F32)


def nn(a, b):
    return lax.dot_general(a, b, (((1,), (0,)), ((), ())), preferred_element_type=F32)


def tn(a, b):
    return lax.dot_general(a, b, (((0,), (0,)), ((), ())), preferred_element_type=F32)

def wrapped(index, size):
    return lax.rem(index + size, size)


def greet(ring, heads_axis):
    barrier = pltpu.get_barrier_semaphore()
    me = lax.axis_index("ctx")
    count = 0
    for s in range(1, STEPS):
        for other in (me + s, me - s):
            pl.semaphore_signal(
                barrier, inc=1, device_id={"ctx": wrapped(other, ring)}, device_id_type=MESH
            )
            count += 1
    mine = lax.axis_index("head")
    for j in range(1, heads_axis):
        pl.semaphore_signal(
            barrier,
            inc=1,
            device_id={"head": lax.rem(mine + j, heads_axis)},
            device_id_type=MESH,
        )
        count += 1
    return lambda: pl.semaphore_wait(barrier, count)


def collect(ring, codes_ref, exps_ref, rope_ref, order_ref, out, send_sem, recv_sem):
    met = greet(ring, 1)
    tokens, width = codes_ref.shape
    rope = rope_ref.shape[0]
    groups = exps_ref.shape[0]
    part = width // groups
    exps = exps_ref[...]
    scale = jnp.where(
        exps == -2, 0.25, jnp.where(exps == -1, 0.5, jnp.where(exps == 0, 1.0, 2.0))
    ).astype(F32)
    scale = jnp.concatenate([scale, jnp.zeros((8 - groups, tokens), F32)], axis=0).T
    for j in range(groups):
        span = slice(j * part, (j + 1) * part)
        out[0, :, span] = (codes_ref[:, span].astype(F32) * scale[:, j : j + 1]).astype(BF16)
    place = jnp.full((tokens, rope), order_ref[0], jnp.int32).astype(F32)
    out[0, :, width:] = jnp.concatenate([rope_ref[...].astype(F32).T, place], axis=1).astype(BF16)
    met()
    me = lax.axis_index("ctx")
    copies = []
    for s in (3, 2, 1):
        copy = pltpu.make_async_remote_copy(
            src_ref=out.at[0],
            dst_ref=out.at[s],
            send_sem=send_sem.at[s],
            recv_sem=recv_sem.at[s],
            device_id={"ctx": wrapped(me + s, ring)},
            device_id_type=MESH,
        )
        copy.start()
        copies.append(copy)
    for copy in copies:
        copy.wait()


def bring_home(
    sizes,
    dlat_ref,
    drope_ref,
    latent_out,
    rope_out,
    parts,
    landed,
    summed,
    send_sem,
    recv_sem,
    head_send,
    head_recv,
):
    ring, heads_axis, factor = sizes
    met = greet(ring, heads_axis)
    tokens, width = latent_out.shape
    rope = rope_out.shape[0]
    me = lax.axis_index("ctx")
    mine = lax.axis_index("head")
    for s in range(1, STEPS):
        rows = pl.ds(s * tokens, tokens)
        parts[s, :, :width] = dlat_ref[rows, :].astype(BF16)
        parts[s, :, width:] = drope_ref[rows, :].astype(BF16)
    met()
    spans = [pl.ds(k * (tokens // 2), tokens // 2) for k in range(2)]
    copies = []
    for k, span in enumerate(spans):
        for s in (3, 2, 1):
            copy = pltpu.make_async_remote_copy(
                src_ref=parts.at[s, span],
                dst_ref=landed.at[s, span],
                send_sem=send_sem.at[k, s],
                recv_sem=recv_sem.at[k, s],
                device_id={"ctx": wrapped(me - s, ring)},
                device_id_type=MESH,
            )
            copy.start()
            copies.append(copy)
    exchanges = []
    for k, span in enumerate(spans):
        for copy in copies[k * (STEPS - 1) : (k + 1) * (STEPS - 1)]:
            copy.wait()
        lat_total = dlat_ref[span, :]
        rope_total = drope_ref[span, :]
        for s in range(1, STEPS):
            lat_total = lat_total + landed[s, span, :width].astype(F32)
            rope_total = rope_total + landed[s, span, width:].astype(F32)
        summed[mine, span, :width] = lat_total.astype(BF16)
        summed[mine, span, width:] = rope_total.astype(BF16)
        for j in range(1, heads_axis):
            copy = pltpu.make_async_remote_copy(
                src_ref=summed.at[mine, span],
                dst_ref=summed.at[mine, span],
                send_sem=head_send.at[k, j],
                recv_sem=head_recv.at[k, j],
                device_id={"head": lax.rem(mine + j, heads_axis)},
                device_id_type=MESH,
            )
            copy.start()
            exchanges.append(copy)
    for copy in exchanges:
        copy.wait()
    total = summed[0].astype(F32)
    for j in range(1, heads_axis):
        total = total + summed[j].astype(F32)
    latent_out[...] = total[:, :width]
    tail = total[:, width:].T
    rope_out[...] = (tail[:rope] + tail[rope:]) * factor


def attend(
    dims,
    packs,
    q_ref,
    qr_ref,
    g_ref,
    uk_ref,
    uv_ref,
    dq_ref,
    dqr_ref,
    dlat_ref,
    drope_ref,
    lat,
    rope_even,
    rope_odd,
    bias,
):
    tokens, width, nope, rope, group = dims
    step = pl.program_id(0)
    factor = 1.0 / math.sqrt(nope + rope)
    log2_scale = factor * math.log2(math.e)

    @pl.when(step == 0)
    def _():
        lane = lax.broadcasted_iota(jnp.int32, (tokens, 2 * rope), 1)
        row = lax.broadcasted_iota(jnp.int32, (tokens, tokens), 0).astype(F32)
        col = lax.broadcasted_iota(jnp.int32, (tokens, tokens), 1).astype(F32)
        own = None
        for s in range(STEPS):
            rows = pl.ds(s * tokens, tokens)
            lat[rows, :] = packs[s, :, :width]
            tail = packs[s, :, width:].astype(F32)
            turned = pltpu.roll(tail, rope, 1)
            rope_even[rows, :] = jnp.where(lane < rope, tail, 0.0).astype(BF16)
            rope_odd[rows, :] = jnp.where(lane >= rope, turned, 0.0).astype(BF16)
            place = jnp.broadcast_to(tail[:, rope : rope + 1], (tokens, tokens)) * tokens
            if s == 0:
                own = place
            bias[rows, :] = jnp.where(place + row <= own + col, 0.0, -jnp.inf)
        dlat_ref[...] = jnp.zeros_like(dlat_ref)
        drope_ref[...] = jnp.zeros_like(drope_ref)

    latent = lat[...]
    lane_q = lax.broadcasted_iota(jnp.int32, (tokens, 2 * rope), 1)
    for pair in range(group // 2):
        first, second = 2 * pair, 2 * pair + 1
        qr = qr_ref[:, pair * 2 * rope : (pair + 1) * 2 * rope]
        keys = nn(latent, jnp.concatenate([uk_ref[first], uk_ref[second]], axis=1)).astype(BF16)
        q = [q_ref[:, h * nope : (h + 1) * nope] for h in (first, second)]
        g = [g_ref[:, h * nope : (h + 1) * nope] for h in (first, second)]
        q_lat = [(nt(uk_ref[h], q[i]) * factor).astype(BF16) for i, h in enumerate((first, second))]
        g_lat = [nt(uv_ref[h], g[i]).astype(BF16) for i, h in enumerate((first, second))]
        dp_both = nn(latent, jnp.concatenate(g_lat, axis=1))
        left = []
        right = []
        turned = None
        scores = []
        for i in range(2):
            full_keys = jnp.concatenate(
                [keys[:, i * nope : (i + 1) * nope], (rope_even, rope_odd)[i][...]], axis=1
            )
            raw = nt(full_keys, jnp.concatenate([q[i], qr], axis=1))
            score = raw * log2_scale + bias[...]
            top = jnp.max(score, axis=0, keepdims=True)
            weight = jnp.exp2(score - top)
            inverse = 1.0 / jnp.sum(weight, axis=0, keepdims=True)
            dp = dp_both[:, i * tokens : (i + 1) * tokens]
            delta = jnp.sum(weight * dp, axis=0, keepdims=True) * inverse
            prob = weight * inverse
            ds = (prob * (dp - delta)).astype(BF16)
            scores.append(ds)
            left += [ds, prob.astype(BF16)]
            right += [q_lat[i], g_lat[i]]
            grad = tn(full_keys, ds).T * factor
            h = (first, second)[i]
            dq_ref[:, h * nope : (h + 1) * nope] = grad[:, :nope].astype(BF16)
            turned = grad[:, nope:] if turned is None else turned + grad[:, nope:]
        dqr_ref[:, pair * 2 * rope : (pair + 1) * 2 * rope] = turned.astype(BF16)
        dlat_ref[...] += nt(jnp.concatenate(left, axis=1), jnp.concatenate(right, axis=1))
        zero = jnp.zeros_like(qr)
        qr_split = jnp.concatenate(
            [jnp.where(lane_q < rope, qr, zero), jnp.where(lane_q >= rope, qr, zero)], axis=0
        )
        drope_ref[...] += nn(jnp.concatenate(scores, axis=1), qr_split)


def body(
    query_nope,
    query_rope,
    out_grad,
    latent_codes,
    scale_exponents,
    key_rope,
    block_order,
    up_keys,
    up_values,
):
    tokens, width = latent_codes.shape
    heads, _, nope = up_keys.shape
    rope = key_rope.shape[1]
    group = 8
    factor = 1.0 / math.sqrt(nope + rope)
    ring = lax.axis_size("ctx")
    heads_axis = lax.axis_size("head")
    vmem = pl.BlockSpec(memory_space=pltpu.VMEM)
    packs = pl.pallas_call(
        functools.partial(collect, ring),
        out_shape=jax.ShapeDtypeStruct((STEPS, tokens, width + 2 * rope), BF16),
        in_specs=[vmem] * 3 + [pl.BlockSpec(memory_space=pltpu.SMEM)],
        out_specs=vmem,
        scratch_shapes=[pltpu.SemaphoreType.DMA((STEPS,)), pltpu.SemaphoreType.DMA((STEPS,))],
        compiler_params=pltpu.CompilerParams(collective_id=0, has_side_effects=True),
    )(latent_codes, scale_exponents.T, key_rope.T, block_order)
    keys = STEPS * tokens
    whole = lambda i: (0, 0)
    cols = lambda i: (0, i)
    per_head = lambda i: (i, 0, 0)
    grad_nope, grad_rope, dlat, drope = pl.pallas_call(
        functools.partial(attend, (tokens, width, nope, rope, group)),
        grid=(heads // group,),
        in_specs=[pl.BlockSpec((STEPS, tokens, width + 2 * rope), lambda i: (0, 0, 0))]
        + [
            pl.BlockSpec((tokens, group * nope), cols),
            pl.BlockSpec((tokens, group * rope), cols),
            pl.BlockSpec((tokens, group * nope), cols),
            pl.BlockSpec((group, width, nope), per_head),
            pl.BlockSpec((group, width, nope), per_head),
        ],
        out_specs=[
            pl.BlockSpec((tokens, group * nope), cols),
            pl.BlockSpec((tokens, group * rope), cols),
            pl.BlockSpec((keys, width), whole),
            pl.BlockSpec((keys, 2 * rope), whole),
        ],
        out_shape=[
            jax.ShapeDtypeStruct((tokens, heads * nope), BF16),
            jax.ShapeDtypeStruct((tokens, heads * rope), BF16),
            jax.ShapeDtypeStruct((keys, width), F32),
            jax.ShapeDtypeStruct((keys, 2 * rope), F32),
        ],
        scratch_shapes=[
            pltpu.VMEM((keys, width), BF16),
            pltpu.VMEM((keys, 2 * rope), BF16),
            pltpu.VMEM((keys, 2 * rope), BF16),
            pltpu.VMEM((keys, tokens), F32),
        ],
        compiler_params=pltpu.CompilerParams(
            dimension_semantics=("arbitrary",), vmem_limit_bytes=60 * 2**20
        ),
    )(packs, query_nope, query_rope, out_grad, up_keys, up_values)
    block = (tokens, width + 2 * rope)
    grad_latent, grad_rope_keys = pl.pallas_call(
        functools.partial(bring_home, (ring, heads_axis, factor)),
        out_shape=[
            jax.ShapeDtypeStruct((tokens, width), F32),
            jax.ShapeDtypeStruct((rope, tokens), F32),
        ],
        in_specs=[vmem, vmem],
        out_specs=[vmem, vmem],
        scratch_shapes=[
            pltpu.VMEM((STEPS,) + block, BF16),
            pltpu.VMEM((STEPS,) + block, BF16),
            pltpu.VMEM((heads_axis,) + block, BF16),
            pltpu.SemaphoreType.DMA((2, STEPS)),
            pltpu.SemaphoreType.DMA((2, STEPS)),
            pltpu.SemaphoreType.DMA((2, heads_axis)),
            pltpu.SemaphoreType.DMA((2, heads_axis)),
        ],
        compiler_params=pltpu.CompilerParams(
            collective_id=1, has_side_effects=True, vmem_limit_bytes=16 * 2**20
        ),
    )(dlat, drope)
    return (grad_nope, grad_rope, grad_latent, grad_rope_keys.T)


def solution(mesh):
    return jax.shard_map(
        body,
        mesh=mesh,
        in_specs=(
            P("ctx", "head"),
            P("ctx", "head"),
            P("ctx", "head"),
            P("ctx", None),
            P("ctx", None),
            P("ctx", None),
            P("ctx"),
            P("head", None, None),
            P("head", None, None),
        ),
        out_specs=(P("ctx", "head"), P("ctx", "head"), P("ctx", None), P("ctx", None)),
        check_vma=False,
    )
```
